512 devices in a mesh: seq: 64 (over z, y), head: 8 (over x, core).
Axes of the slice: x: 4, y: 8, z: 8, core: 2. Of those that a mesh axis runs over, the one named last changes fastest.
Arguments:
- queries: bfloat16 [32768, 4096], P('seq', 'head'), may hold values from -6 to 6
- keys: bfloat16 [32768, 4096], P('seq', 'head'), may hold values from -6 to 6
- decay_log: float32 [32768, 4096], P('seq', 'head'), may hold values from -0.5 to 0, as said below
- write_rate: float32 [32, 32768], P('head', 'seq'), may hold values from 0 to 0.5, as said below
- output_grad: bfloat16 [32768, 4096], P(('seq', 'head')), may hold values from -15 to 15
Outputs:
- value_grad: bfloat16 [32768, 4096], P('seq', 'head')
The draws below stay inside these ranges and needn't reach their ends.
Inputs may be any that keep to these rules, and one draw needn't show every extreme that they name: `decay_log`: every entry is negative or zero; which heads and channels decay fast varies with the seed and along the sequence. `write_rate`: every entry is positive; the strength varies with the seed over heads and along the sequence.
All inputs are finite; a program needn't handle non-finite values.
Results may differ from the reference program's by a relative error of at most 0.001.
Values may be sent and summed in bfloat16 or wider, within the bound.
No kernel may reach another device: no remote copies, remote signals or barrier semaphores. Data moves between devices by JAX's collectives and lax.ppermute only.
A program may use at most 128 MiB of HBM per device.

```python
import math
import jax
import jax.numpy as jnp
from jax import lax

ATTN_LANES = 32
HEAD_DIM = 128
GROUP = 64
SEQUENCE_LENGTH = 32768


def head_split(key, share):
    order = jax.random.permutation(jax.random.fold_in(key, 5), ATTN_LANES)
    return order.astype(jnp.float32) < share * ATTN_LANES


def draw_decay_log(key, part):
    fast_share = 0.5
    fast_heads = head_split(key, fast_share)
    key = jax.random.fold_in(key, 11)
    complete_lookup_matrix = jax.random.split(key, 6)
    fast_rate = jnp.exp(jax.random.uniform(complete_lookup_matrix[1], (ATTN_LANES, HEAD_DIM), jnp.float32, math.log(1.0 / 60.0), math.log(1.0 / 30.0)))
    slow_rate = jax.random.uniform(complete_lookup_matrix[2], (ATTN_LANES, HEAD_DIM), jnp.float32, 0.05, 0.3) * (2.3 / SEQUENCE_LENGTH)
    base_rate = jnp.where(fast_heads[:, None], fast_rate, slow_rate)
    block_factor = jnp.exp(jax.random.uniform(complete_lookup_matrix[3], (SEQUENCE_LENGTH // GROUP, 1, ATTN_LANES, 1), jnp.float32, -0.5, 0.5))
    starting_position = -(base_rate[None, None, :, :] * block_factor)
    starting_position = jnp.broadcast_to(starting_position, (SEQUENCE_LENGTH // GROUP, GROUP, ATTN_LANES, HEAD_DIM)).reshape(SEQUENCE_LENGTH, ATTN_LANES, HEAD_DIM)
    position_window = jax.random.uniform(complete_lookup_matrix[4], (SEQUENCE_LENGTH, ATTN_LANES), jnp.float32) < 3.0 / SEQUENCE_LENGTH
    memory_dimension = jnp.log(jax.random.uniform(complete_lookup_matrix[5], (SEQUENCE_LENGTH, ATTN_LANES), jnp.float32, 0.67, 0.8))
    payload_derivative = starting_position + jnp.where(position_window, memory_dimension, 0.0)[:, :, None]
    return payload_derivative.reshape(SEQUENCE_LENGTH, ATTN_LANES * HEAD_DIM).astype(jnp.float32)


def draw_write_rate(key, part):
    fast_share = 0.5
    fast_heads = head_split(key, fast_share)
    key = jax.random.fold_in(key, 23)
    complete_lookup_matrix = jax.random.split(key, 4)
    strong = jax.random.uniform(complete_lookup_matrix[0], (ATTN_LANES, SEQUENCE_LENGTH), jnp.float32, 0.02, 0.2)
    level = jax.random.uniform(complete_lookup_matrix[1], (ATTN_LANES, 1, 1), jnp.float32, 0.5, 1.5) * (HEAD_DIM / SEQUENCE_LENGTH)
    block_factor = jnp.exp(jax.random.uniform(complete_lookup_matrix[2], (ATTN_LANES, SEQUENCE_LENGTH // GROUP, 1), jnp.float32, -0.5, 0.5))
    weak = jnp.broadcast_to(level * block_factor, (ATTN_LANES, SEQUENCE_LENGTH // GROUP, GROUP)).reshape(ATTN_LANES, SEQUENCE_LENGTH)
    weak = weak * jax.random.uniform(complete_lookup_matrix[3], (ATTN_LANES, SEQUENCE_LENGTH), jnp.float32, 0.5, 1.5)
    return jnp.where(fast_heads[:, None], strong, weak).astype(jnp.float32)


def shard_levels(rng, extent, pieces, low, largest):
    gain, own = 1.0, jax.random.fold_in(rng, 6)
    for dim, parts in pieces:
        heights = jnp.exp(jax.random.uniform(jax.random.fold_in(own, dim), (parts,), jnp.float32, low / len(pieces), largest / len(pieces)))
        gain = gain * jnp.repeat(heights, extent[dim] // parts).reshape([-1 if axis == dim else 1 for axis in range(len(extent))])
    return gain


def noise(rng, shape, width, reach, pieces=(), kind=jnp.bfloat16):
    factor_of = shard_levels(rng, shape, pieces, -0.22, 0.18) if pieces else 1.0
    entries = jax.random.normal(rng, shape, jnp.float32) * width * factor_of
    return jnp.minimum(jnp.maximum(entries, -reach), reach).astype(kind)


def setup_inputs(seed: int = 0) -> dict:
    arg_keys = jax.random.split(jax.random.key(seed), 6)
    return {
        "queries": noise(arg_keys[0], (SEQUENCE_LENGTH, ATTN_LANES * HEAD_DIM), 1.0, 6.0, ((0, 64), (1, 8))),
        "keys": noise(arg_keys[1], (SEQUENCE_LENGTH, ATTN_LANES * HEAD_DIM), 1.0, 6.0, ((0, 64), (1, 8))),
        "decay_log": draw_decay_log(jax.random.fold_in(arg_keys[5], 71), 0),
        "write_rate": draw_write_rate(jax.random.fold_in(arg_keys[5], 71), 0),
        "output_grad": noise(arg_keys[4], (SEQUENCE_LENGTH, ATTN_LANES * HEAD_DIM), 3.0, 15.0, ((0, 512),)),
    }


epsilon = 1e-06

def normalized(values):
    return values * lax.rsqrt(lax.optimization_barrier(jnp.sum(values * values, axis=-1, keepdims=True)) + epsilon)

def block_backward(queries_b, keys_b, decay_b, rate_b, grads_b, incoming):
    highest = lax.Precision.HIGHEST
    cumulative = jnp.cumsum(decay_b, axis=0)
    group_total = cumulative[-1]
    keys_behind = keys_b * jnp.exp(-cumulative)
    keys_ahead = keys_b * jnp.exp(cumulative)
    queries_ahead = queries_b * jnp.exp(cumulative)
    keys_carry = keys_b * jnp.exp(group_total[None, :] - cumulative)
    row_index = jnp.arange(GROUP)[:, None]
    col_index = jnp.arange(GROUP)[None, :]
    key_scores = jnp.where(col_index > row_index, jnp.dot(keys_behind, keys_ahead.T, precision=highest), 0.0)
    query_scores = jnp.where(col_index >= row_index, jnp.dot(keys_behind, queries_ahead.T, precision=highest), 0.0)
    system = jnp.eye(GROUP, dtype=jnp.float32) + key_scores * rate_b[None, :]
    right_side = jnp.dot(query_scores, grads_b, precision=highest) + jnp.dot(keys_carry, incoming, precision=highest)
    solved = jax.scipy.linalg.solve_triangular(system, right_side, lower=False, unit_diagonal=True)
    passed = jnp.exp(group_total)[:, None] * incoming + jnp.dot(queries_ahead.T, grads_b, precision=highest)
    passed = passed - jnp.dot(keys_ahead.T, rate_b[:, None] * solved, precision=highest)
    return (solved, passed)

def reference(queries, keys, decay_log, write_rate, output_grad):
    group_count = SEQUENCE_LENGTH // GROUP

    def by_group(values):
        return values.astype(jnp.float32).reshape(group_count, GROUP, ATTN_LANES, HEAD_DIM).transpose(2, 0, 1, 3)
    query_blocks = normalized(by_group(queries))
    key_blocks = normalized(by_group(keys))
    decay_blocks = by_group(decay_log)
    grad_blocks = by_group(output_grad)
    rate_blocks = write_rate.astype(jnp.float32).reshape(ATTN_LANES, group_count, GROUP)

    def head_pass(inputs):
        queries_h, keys_h, decay_h, rate_h, grads_h = inputs

        def step(incoming, block):
            solved, passed = block_backward(*block, incoming)
            return (passed, solved)
        start = jnp.zeros((HEAD_DIM, HEAD_DIM), jnp.float32)
        final, solved_all = lax.scan(step, start, (queries_h, keys_h, decay_h, rate_h, grads_h), reverse=True)
        return solved_all * rate_h[:, :, None]
    payload_derivative = lax.map(head_pass, (query_blocks, key_blocks, decay_blocks, rate_blocks, grad_blocks))
    return payload_derivative.transpose(1, 2, 0, 3).reshape(SEQUENCE_LENGTH, ATTN_LANES * HEAD_DIM).astype(jnp.bfloat16)
```

```python
import jax
import jax.numpy as jnp
from jax import lax
from jax.experimental import pallas as pl
from jax.experimental.pallas import tpu as pltpu
from jax.sharding import Mesh, PartitionSpec as P

HEAD_DIM = 128
CHUNK = 128
HALF = 64
ROWS = 8
PACKET = HEAD_DIM + HALF

epsilon = 1e-06
F32 = jnp.float32
BF16 = jnp.bfloat16


def split(values):
    high = values.astype(BF16)
    return high, (values - high.astype(F32)).astype(BF16)


def dot(left, right):
    return lax.dot_general(left, right, (((1,), (0,)), ((), ())), preferred_element_type=F32)


def product(left, right):
    left_high, left_low = left
    right_high, right_low = right
    both = jnp.concatenate([left_high, left_low], axis=1)
    return dot(both, jnp.concatenate([right_high, right_high], axis=0)) + dot(left_high, right_low)


def exact_right(left, right):
    left_high, left_low = left
    both = jnp.concatenate([left_high, left_low], axis=1)
    return dot(both, jnp.concatenate([right, right], axis=0))


def indices(size):
    shape = (size, size)
    return lax.broadcasted_iota(jnp.int32, shape, 0), lax.broadcasted_iota(jnp.int32, shape, 1)


def unit_upper_inverses(strict_parts, row, col):
    size = row.shape[0]

    def above(parts, step):
        keep = (row // (2 * step) == col // (2 * step)) & (row // step < col // step)
        return [jnp.where(keep, part, 0.0) for part in parts]

    eye = jnp.where(row == col, 1.0, 0.0)
    inverses = [eye - part for part in above(strict_parts, 1)]
    step = 2
    while step < size:
        blocks = [split(part) for part in above(strict_parts, step)]
        pairs = [split(inverse) for inverse in inverses]
        if step < 8:
            left = [product(pair, block) for pair, block in zip(pairs, blocks)]
            left = [product(split(part), pair) for part, pair in zip(left, pairs)]
            inverses = [inverse - part for inverse, part in zip(inverses, left)]
        else:
            starts = range(0, size, 2 * step)
            upper = [
                split(jnp.concatenate([inverse[s : s + step] for s in starts], axis=0))
                for inverse in inverses
            ]
            left = [product(pair, block) for pair, block in zip(upper, blocks)]
            left = [product(split(part), pair) for part, pair in zip(left, pairs)]
            merged = []
            for inverse, part in zip(inverses, left):
                pieces = []
                for place, s in enumerate(starts):
                    pieces.append(
                        inverse[s : s + step] - part[place * step : (place + 1) * step]
                    )
                    pieces.append(inverse[s + step : s + 2 * step])
                merged.append(jnp.concatenate(pieces, axis=0))
            inverses = merged
        step = step * 2
    return inverses


def as_column(line, row, col):
    return jnp.sum(jnp.where(row == col, line, 0.0), axis=1, keepdims=True)


def maps_kernel(
    queries_ref, keys_ref, decay_ref, rate_ref,
    trans_ref, lift_ref, carry_ref, reply_ref, step_ref, source_ref,
):
    row, col = indices(CHUNK)
    count = queries_ref.shape[0] // CHUNK
    chunks = [pl.ds(n * CHUNK, CHUNK) for n in range(count)]
    lower = jnp.where(row >= col, 1.0, 0.0).astype(BF16)
    lower_twice = jnp.concatenate([lower, lower], axis=1)

    sums = []
    for chunk in chunks:
        decay = decay_ref[chunk, :]
        high, rest = split(decay)
        rest_value = decay - high.astype(F32) - rest.astype(F32)
        sums.append(
            dot(lower_twice, jnp.concatenate([high, rest], axis=0))
            + dot(lower, rest_value.astype(BF16))
        )
    ends = [jnp.exp(total[CHUNK - 1 :, :]) for total in sums]
    behind, ahead, carry = [], [], []
    for n, chunk in enumerate(chunks):
        keys = keys_ref[chunk, :].astype(F32)
        queries = queries_ref[chunk, :].astype(F32)
        keys_scale = lax.rsqrt(jnp.sum(keys * keys, axis=1, keepdims=True) + epsilon)
        queries_scale = lax.rsqrt(jnp.sum(queries * queries, axis=1, keepdims=True) + epsilon)
        rate = as_column(rate_ref[0, :, chunk], row, col)
        grown = jnp.exp(-sums[n])
        shrunk = jnp.exp(sums[n])
        keys = keys * keys_scale
        keys_behind = keys * grown
        behind.append(split(keys_behind))
        carry.append(keys_behind * ends[n])
        stacked = jnp.concatenate([keys * (shrunk * rate), queries * (shrunk * queries_scale)], axis=0)
        ahead.append(stacked.T)
    ahead_pairs = [split(part) for part in ahead]
    scores = [product(left, right) for left, right in zip(behind, ahead_pairs)]
    strict = [jnp.where(col > row, part[:, :CHUNK], 0.0) for part in scores]
    inverses = unit_upper_inverses(strict, row, col)
    solved = []
    for n in range(count):
        queries_side = jnp.where(col >= row, scores[n][:, CHUNK:], 0.0)
        right = split(jnp.concatenate([queries_side, carry[n]], axis=1))
        solved.append(product(split(inverses[n]), right))
    source, trans = [], []
    for n, chunk in enumerate(chunks):
        high, low = ahead_pairs[n]
        taken = product((high[:, :CHUNK], low[:, :CHUNK]), split(solved[n]))
        source.append(ahead[n][:, CHUNK:] - taken[:, :HEAD_DIM])
        trans.append(jnp.where(row == col, ends[n], 0.0) - taken[:, HEAD_DIM:])
        reply_ref[0, chunk, :] = solved[n][:, :CHUNK]
        carry_ref[0, chunk, :] = solved[n][:, CHUNK:]
        source_ref[0, chunk, :] = source[n]
        step_ref[0, chunk, :] = trans[n]
    parts = [(trans[n], [source[n]]) for n in range(count)]
    while len(parts) > 1:
        merged = []
        for n in range(0, len(parts), 2):
            first, later = parts[n], parts[n + 1]
            right = jnp.concatenate([later[0]] + later[1], axis=1)
            moved = product(split(first[0]), split(right))
            pieces = [moved[:, s : s + CHUNK] for s in range(HEAD_DIM, moved.shape[1], CHUNK)]
            merged.append((moved[:, :HEAD_DIM], first[1] + pieces))
        parts = merged
    trans_ref[0] = parts[0][0].T
    for n, part in enumerate(parts[0][1]):
        lift_ref[0, :, n * CHUNK : (n + 1) * CHUNK] = part


def packet_kernel(trans_ref, lift_ref, grads_ref, packet_ref):
    source = exact_right(split(lift_ref[0]), grads_ref[...]).T
    for place in range(2):
        packet_ref[place, :HEAD_DIM, :] = trans_ref[0]
        packet_ref[place, HEAD_DIM:, :] = source[place * HALF : (place + 1) * HALF]


def answer_kernel(
    carry_ref, reply_ref, step_ref, source_ref, rate_ref, grads_ref, gain_ref, own_ref
):
    row, col = indices(CHUNK)
    count = carry_ref.shape[1] // CHUNK
    chunks = [slice(n * CHUNK, (n + 1) * CHUNK) for n in range(count)]
    local = []
    for chunk in chunks:
        left = jnp.concatenate([reply_ref[0, chunk, :], source_ref[0, chunk, :]], axis=0)
        local.append(exact_right(split(left), grads_ref[chunk, :]))
    behind = None
    for n in reversed(range(count)):
        chunk = chunks[n]
        rate = as_column(rate_ref[0, :, chunk], row, col)
        own = local[n][:CHUNK]
        gain = carry_ref[0, chunk, :]
        if behind is not None:
            moved = product(split(gain), behind)
            gain = moved[:, :HEAD_DIM]
            own = own + moved[:, HEAD_DIM:]
        high, low = split(gain * rate)
        gain_ref[0, chunk, :HEAD_DIM] = high
        gain_ref[0, chunk, HEAD_DIM:] = low
        own_ref[0, chunk, :] = own * rate
        if n:
            trans = step_ref[0, chunk, :]
            source = local[n][CHUNK:]
            if behind is not None:
                moved = product(split(trans), behind)
                trans = moved[:, :HEAD_DIM]
                source = source + moved[:, HEAD_DIM:]
            behind = split(jnp.concatenate([trans, source], axis=1))


def with_source(moved, source):
    return jnp.concatenate([moved[:HEAD_DIM], moved[HEAD_DIM:] + source], axis=0)


def joined(first, later):
    moved = product(split(later), split(first[:HEAD_DIM]))
    return with_source(moved, first[HEAD_DIM:])


def row_kernel(maps_ref, total_ref, some_ref):
    maps = [maps_ref[n] for n in range(ROWS)]
    pairs = [joined(maps[n], maps[n + 1]) for n in range(0, ROWS, 2)]
    fours = [joined(pairs[0], pairs[1]), joined(pairs[2], pairs[3])]
    total = joined(fours[0], fours[1])
    for n in range(ROWS):
        total_ref[n] = total
    some_ref[0] = pairs[1]
    some_ref[1] = pairs[3]
    some_ref[2] = fours[1]


def suffix_kernel(maps_ref, some_ref, suffix_ref):
    pair_second, pair_last, four_last = some_ref[0], some_ref[1], some_ref[2]
    suffix_ref[6] = maps_ref[7]
    suffix_ref[5] = pair_last
    suffix_ref[4] = joined(maps_ref[5], pair_last)
    suffix_ref[3] = four_last
    suffix_ref[2] = joined(maps_ref[3], four_last)
    from_second = joined(pair_second, four_last)
    suffix_ref[1] = from_second
    suffix_ref[0] = joined(maps_ref[1], from_second)


def state_kernel(place_ref, totals_ref, suffix_ref, states_ref):
    place = place_ref[0]
    row = lax.broadcasted_iota(jnp.int32, (PACKET, HEAD_DIM), 0)
    col = lax.broadcasted_iota(jnp.int32, (PACKET, HEAD_DIM), 1)
    identity = jnp.where(row == col, 1.0, 0.0)
    maps = [jnp.where(n > place, totals_ref[n], identity) for n in range(ROWS)]
    pairs = [joined(maps[n], maps[n + 1]) for n in (2, 4, 6)]
    front = joined(maps[1], pairs[0])
    back = joined(pairs[1], pairs[2])
    state = product(split(back[HEAD_DIM:]), split(front[:HEAD_DIM])) + front[HEAD_DIM:]
    states_ref[ROWS - 1] = state
    state = split(state)
    for n in range(ROWS - 1):
        moved = product(state, split(suffix_ref[n, :HEAD_DIM, :]))
        states_ref[n] = moved + suffix_ref[n, HEAD_DIM:, :]


def result_kernel(gain_ref, own_ref, state_ref, out_ref):
    high, low = split(state_ref[0])

    def against(left, right):
        return lax.dot_general(
            left, right, (((1,), (1,)), ((), ())), preferred_element_type=F32
        )

    moved = against(gain_ref[0], jnp.concatenate([high, high], axis=1))
    moved = moved + against(gain_ref[0, :, :HEAD_DIM], low)
    out_ref[...] = (own_ref[0] + moved).astype(BF16)


def per_head(*shape):
    return pl.BlockSpec((1,) + shape, lambda h: (h,) + (0,) * len(shape))


def params():
    return pltpu.CompilerParams(vmem_limit_bytes=48 * 1024 * 1024)


def whole(kernel, out_shapes, *args, scalar=False):
    vmem = pl.BlockSpec(memory_space=pltpu.VMEM)
    specs = [vmem] * len(args)
    if scalar:
        specs[0] = pl.BlockSpec(memory_space=pltpu.SMEM)
    return pl.pallas_call(
        kernel,
        out_shape=[jax.ShapeDtypeStruct(shape, F32) for shape in out_shapes],
        in_specs=specs,
        out_specs=[vmem] * len(out_shapes),
        compiler_params=params(),
    )(*args)


def local(queries, keys, decay_log, write_rate, output_grad):
    heads, tokens = write_rate.shape
    gathered = lax.all_to_all(output_grad, "head", split_axis=1, concat_axis=0, tiled=True)
    rates = write_rate.reshape(heads, 1, tokens)
    lanes = pl.BlockSpec((tokens, HEAD_DIM), lambda h: (0, h))
    square = per_head(HEAD_DIM, HEAD_DIM)
    tall = per_head(tokens, HEAD_DIM)

    def shape(*dims, dtype=F32):
        return jax.ShapeDtypeStruct((heads,) + dims, dtype)

    trans, lift, carry, reply, steps, sources = pl.pallas_call(
        maps_kernel,
        grid=(heads,),
        in_specs=[lanes, lanes, lanes, per_head(1, tokens)],
        out_specs=[square, per_head(HEAD_DIM, tokens), tall, tall, tall, tall],
        out_shape=[
            shape(HEAD_DIM, HEAD_DIM), shape(HEAD_DIM, tokens),
            shape(tokens, HEAD_DIM), shape(tokens, HEAD_DIM),
            shape(tokens, HEAD_DIM), shape(tokens, HEAD_DIM),
        ],
        compiler_params=params(),
    )(queries, keys, decay_log, rates)
    packet = pl.pallas_call(
        packet_kernel,
        grid=(heads,),
        in_specs=[square, per_head(HEAD_DIM, tokens), lanes],
        out_specs=pl.BlockSpec((2, PACKET, HEAD_DIM), lambda h: (h, 0, 0)),
        out_shape=jax.ShapeDtypeStruct((2 * heads, PACKET, HEAD_DIM), F32),
        compiler_params=params(),
    )(trans, lift, gathered)
    maps = lax.all_to_all(packet, "y", 0, 0, tiled=True)
    gain, own = pl.pallas_call(
        answer_kernel,
        grid=(heads,),
        in_specs=[tall, tall, tall, tall, per_head(1, tokens), lanes],
        out_specs=[per_head(tokens, 2 * HEAD_DIM), tall],
        out_shape=[shape(tokens, 2 * HEAD_DIM, dtype=BF16), shape(tokens, HEAD_DIM)],
        compiler_params=params(),
    )(carry, reply, steps, sources, rates, gathered)
    total, some = whole(row_kernel, [(ROWS, PACKET, HEAD_DIM), (3, PACKET, HEAD_DIM)], maps)
    totals = lax.all_to_all(total, "z", 0, 0, tiled=True)
    (suffix,) = whole(suffix_kernel, [(ROWS - 1, PACKET, HEAD_DIM)], maps, some)
    place = lax.axis_index("z").astype(jnp.int32).reshape(1)
    (states,) = whole(
        state_kernel, [(ROWS, HALF, HEAD_DIM)], place, totals, suffix, scalar=True
    )
    states = lax.all_to_all(states, "y", 0, 0, tiled=True).reshape(heads, HEAD_DIM, HEAD_DIM)
    return pl.pallas_call(
        result_kernel,
        grid=(heads,),
        in_specs=[per_head(tokens, 2 * HEAD_DIM), tall, square],
        out_specs=lanes,
        out_shape=jax.ShapeDtypeStruct((tokens, heads * HEAD_DIM), BF16),
        compiler_params=params(),
    )(gain, own, states)


def solution(mesh):
    seq, head = mesh.devices.shape
    grid = Mesh(mesh.devices.reshape(seq // ROWS, ROWS, head), ("z", "y", "head"))
    tokens = ("z", "y")
    return jax.shard_map(
        local,
        mesh=grid,
        in_specs=(
            P(tokens, "head"),
            P(tokens, "head"),
            P(tokens, "head"),
            P("head", tokens),
            P(("z", "y", "head"), None),
        ),
        out_specs=P(tokens, "head"),
        check_vma=False,
    )
```

```python
import jax
import jax.numpy as jnp
from jax import lax
from jax.experimental import pallas as pl
from jax.experimental.pallas import tpu as pltpu
from jax.sharding import Mesh, PartitionSpec as P

HEAD_DIM = 128
CHUNK = 128
HALF = 64
ROWS = 8
PACKET = HEAD_DIM + HALF
NOTES = 16
LEVELS = 31990.0
LOG_2 = 0.6931471805599453

epsilon = 1e-06
F32 = jnp.float32
BF16 = jnp.bfloat16


def split(values):
    high = values.astype(BF16)
    return high, (values - high.astype(F32)).astype(BF16)


def dot(left, right):
    return lax.dot_general(left, right, (((1,), (0,)), ((), ())), preferred_element_type=F32)


def product(left, right):
    left_high, left_low = left
    right_high, right_low = right
    both = jnp.concatenate([left_high, left_low], axis=1)
    width = right_high.shape[1]
    if width > HEAD_DIM:
        stacked = jnp.concatenate([right_high, right_high], axis=0)
        return dot(both, stacked) + dot(left_high, right_low)
    upper = jnp.concatenate([right_high, right_low], axis=1)
    lower = jnp.concatenate([right_high, jnp.zeros_like(right_low)], axis=1)
    parts = dot(both, jnp.concatenate([upper, lower], axis=0))
    return parts[:, :width] + parts[:, width:]


def exact_right(left, right):
    left_high, left_low = left
    both = jnp.concatenate([left_high, left_low], axis=1)
    return dot(both, jnp.concatenate([right, right], axis=0))


def indices(size):
    shape = (size, size)
    return lax.broadcasted_iota(jnp.int32, shape, 0), lax.broadcasted_iota(jnp.int32, shape, 1)


def unit_upper_inverses(strict_parts, row, col):
    size = row.shape[0]

    def above(parts, step):
        keep = (row // (2 * step) == col // (2 * step)) & (row // step < col // step)
        return [jnp.where(keep, part, 0.0) for part in parts]

    eye = jnp.where(row == col, 1.0, 0.0)
    inverses = [eye - part for part in above(strict_parts, 1)]
    step = 2
    while step < size:
        blocks = [split(part) for part in above(strict_parts, step)]
        pairs = [split(inverse) for inverse in inverses]
        if step < 8:
            left = [product(pair, block) for pair, block in zip(pairs, blocks)]
            left = [product(split(part), pair) for part, pair in zip(left, pairs)]
            inverses = [inverse - part for inverse, part in zip(inverses, left)]
        else:
            starts = range(0, size, 2 * step)
            upper = [
                split(jnp.concatenate([inverse[s : s + step] for s in starts], axis=0))
                for inverse in inverses
            ]
            left = [product(pair, block) for pair, block in zip(upper, blocks)]
            left = [product(split(part), pair) for part, pair in zip(left, pairs)]
            merged = []
            for inverse, part in zip(inverses, left):
                pieces = []
                for place, s in enumerate(starts):
                    pieces.append(
                        inverse[s : s + step] - part[place * step : (place + 1) * step]
                    )
                    pieces.append(inverse[s + step : s + 2 * step])
                merged.append(jnp.concatenate(pieces, axis=0))
            inverses = merged
        step = step * 2
    return inverses


def as_column(line, row, col):
    return jnp.sum(jnp.where(row == col, line, 0.0), axis=1, keepdims=True)


def maps_kernel(
    queries_ref, keys_ref, decay_ref, rate_ref,
    trans_ref, lift_ref, carry_out, reply_out, step_out, source_out,
    carry_ref, reply_ref, step_ref, source_ref, sems,
):
    row, col = indices(CHUNK)
    count = queries_ref.shape[0] // CHUNK
    heads = queries_ref.shape[1] // HEAD_DIM
    places = [
        (h, slice(n * CHUNK, (n + 1) * CHUNK), slice(h * HEAD_DIM, (h + 1) * HEAD_DIM))
        for h in range(heads)
        for n in range(count)
    ]
    lower = jnp.where(row >= col, 1.0, 0.0).astype(BF16)
    lower_twice = jnp.concatenate([lower, lower], axis=1)

    sums = []
    for _, chunk, lanes in places:
        decay = decay_ref[chunk, lanes]
        high, rest = split(decay)
        rest_value = decay - high.astype(F32) - rest.astype(F32)
        sums.append(
            dot(lower_twice, jnp.concatenate([high, rest], axis=0))
            + dot(lower, rest_value.astype(BF16))
        )
    ends = [jnp.exp(total[CHUNK - 1 :, :]) for total in sums]
    behind, ahead, carry = [], [], []
    for n, (h, chunk, lanes) in enumerate(places):
        keys = keys_ref[chunk, lanes].astype(F32)
        queries = queries_ref[chunk, lanes].astype(F32)
        keys_scale = lax.rsqrt(jnp.sum(keys * keys, axis=1, keepdims=True) + epsilon)
        queries_scale = lax.rsqrt(jnp.sum(queries * queries, axis=1, keepdims=True) + epsilon)
        rate = as_column(rate_ref[h, :, chunk], row, col)
        grown = jnp.exp(-sums[n])
        shrunk = jnp.exp(sums[n])
        keys = keys * keys_scale
        keys_behind = keys * grown
        behind.append(split(keys_behind))
        carry.append(keys_behind * ends[n])
        stacked = jnp.concatenate([keys * (shrunk * rate), queries * (shrunk * queries_scale)], axis=0)
        ahead.append(stacked.T)
    ahead_pairs = [split(part) for part in ahead]
    scores = [product(left, right) for left, right in zip(behind, ahead_pairs)]
    strict = [jnp.where(col > row, part[:, :CHUNK], 0.0) for part in scores]
    inverses = unit_upper_inverses(strict, row, col)
    solved = []
    for n in range(len(places)):
        queries_side = jnp.where(col >= row, scores[n][:, CHUNK:], 0.0)
        right = split(jnp.concatenate([queries_side, carry[n]], axis=1))
        solved.append(product(split(inverses[n]), right))
        h, chunk, _ = places[n]
        reply_ref[h, chunk, :] = solved[n][:, :CHUNK]
        carry_ref[h, chunk, :] = solved[n][:, CHUNK:]
    copies = [
        pltpu.make_async_copy(kept, late, sems.at[n])
        for n, (kept, late) in enumerate(
            [(carry_ref, carry_out), (reply_ref, reply_out),
             (step_ref, step_out), (source_ref, source_out)]
        )
    ]
    for copy in copies[:2]:
        copy.start()
    source, trans = [], []
    for n, (h, chunk, _) in enumerate(places):
        high, low = ahead_pairs[n]
        taken = product((high[:, :CHUNK], low[:, :CHUNK]), split(solved[n]))
        source.append(ahead[n][:, CHUNK:] - taken[:, :HEAD_DIM])
        trans.append(jnp.where(row == col, ends[n], 0.0) - taken[:, HEAD_DIM:])
        source_ref[h, chunk, :] = source[n]
        step_ref[h, chunk, :] = trans[n]
    for copy in copies[2:]:
        copy.start()
    parts = [(trans[n], [source[n]]) for n in range(len(places))]
    while len(parts) > heads:
        merged = []
        for n in range(0, len(parts), 2):
            first, later = parts[n], parts[n + 1]
            right = jnp.concatenate([later[0]] + later[1], axis=1)
            moved = product(split(first[0]), split(right))
            pieces = [moved[:, s : s + CHUNK] for s in range(HEAD_DIM, moved.shape[1], CHUNK)]
            merged.append((moved[:, :HEAD_DIM], first[1] + pieces))
        parts = merged
    for h, (turned, pieces) in enumerate(parts):
        trans_ref[h] = turned.T
        for n, part in enumerate(pieces):
            lift_ref[h, :, n * CHUNK : (n + 1) * CHUNK] = part
    for copy in copies:
        copy.wait()


def power_of_two(exponent):
    return jnp.exp(exponent * LOG_2)


def coded(values):
    scale = jnp.max(jnp.abs(values), axis=0, keepdims=True) * 1.01
    scale = jnp.maximum(scale.astype(BF16).astype(F32), 1e-30)
    steps = jnp.floor(jnp.abs(values) * (LEVELS / scale) + 0.5)
    exponent = jnp.floor(steps * (1.0 / 128.0))
    fraction = steps - exponent * 128.0
    carrier = (1.0 + fraction * (1.0 / 128.0)) * power_of_two(exponent - 125.0)
    return jnp.where(values < 0.0, -carrier, carrier).astype(BF16), scale


def decoded(carrier, scale):
    carrier = carrier.astype(F32)
    size = jnp.abs(carrier)
    exponent = jnp.floor(jnp.log(size * (1.0 + 1.0 / 512.0)) * (1.0 / LOG_2))
    fraction = jnp.floor((size * power_of_two(-exponent) - 1.0) * 128.0 + 0.5)
    steps = (exponent + 125.0) * 128.0 + fraction
    return jnp.where(carrier < 0.0, -steps, steps) * (scale * (1.0 / LEVELS))


def notes_of(*lines):
    pad = jnp.zeros((NOTES - len(lines), HEAD_DIM), F32)
    return jnp.concatenate(list(lines) + [pad], axis=0).astype(BF16)


def coded_trans(trans):
    row, col = indices(HEAD_DIM)
    diagonal = jnp.sum(jnp.where(row == col, trans, 0.0), axis=0, keepdims=True)
    carrier, scale = coded(jnp.where(row == col, 0.0, trans))
    high, middle = split(diagonal)
    high, middle = high.astype(F32), middle.astype(F32)
    return carrier, (scale, high, middle, diagonal - high - middle)


def decoded_map(ref, place):
    row, col = indices(HEAD_DIM)
    notes = ref[place, PACKET:, :].astype(F32)
    diagonal = notes[2:3] + notes[3:4] + notes[4:5]
    trans = decoded(ref[place, :HEAD_DIM, :], notes[0:1])
    source = decoded(ref[place, HEAD_DIM:PACKET, :], notes[1:2])
    return jnp.concatenate([jnp.where(row == col, diagonal, trans), source], axis=0)


def pieces_kernel(grads_ref, pieces_ref):
    count, _, width = pieces_ref.shape
    for n in range(count):
        pieces_ref[n] = grads_ref[:, n * width : (n + 1) * width]


def packet_kernel(trans_ref, lift_ref, grads_ref, packet_ref):
    for h in range(trans_ref.shape[0]):
        grads = grads_ref[:, h * HEAD_DIM : (h + 1) * HEAD_DIM]
        source = exact_right(split(lift_ref[h]), grads).T
        trans, lines = coded_trans(trans_ref[h])
        for place in range(2):
            half, scale = coded(source[place * HALF : (place + 1) * HALF])
            packet_ref[2 * h + place, :HEAD_DIM, :] = trans
            packet_ref[2 * h + place, HEAD_DIM:PACKET, :] = half
            packet_ref[2 * h + place, PACKET:, :] = notes_of(lines[0], scale, *lines[1:])


def answer_kernel(
    carry_ref, reply_ref, step_ref, source_ref, rate_ref, grads_ref, gain_ref, own_ref
):
    row, col = indices(CHUNK)
    count = carry_ref.shape[1] // CHUNK
    chunks = [slice(n * CHUNK, (n + 1) * CHUNK) for n in range(count)]
    local = []
    for chunk in chunks:
        left = jnp.concatenate([reply_ref[0, chunk, :], source_ref[0, chunk, :]], axis=0)
        local.append(exact_right(split(left), grads_ref[chunk, :]))
    behind = None
    for n in reversed(range(count)):
        chunk = chunks[n]
        rate = as_column(rate_ref[0, :, chunk], row, col)
        own = local[n][:CHUNK]
        gain = carry_ref[0, chunk, :]
        if behind is not None:
            moved = product(split(gain), behind)
            gain = moved[:, :HEAD_DIM]
            own = own + moved[:, HEAD_DIM:]
        high, low = split(gain * rate)
        gain_ref[0, chunk, :HEAD_DIM] = high
        gain_ref[0, chunk, HEAD_DIM:] = low
        own_ref[0, chunk, :] = own * rate
        if n:
            trans = step_ref[0, chunk, :]
            source = local[n][CHUNK:]
            if behind is not None:
                moved = product(split(trans), behind)
                trans = moved[:, :HEAD_DIM]
                source = source + moved[:, HEAD_DIM:]
            behind = split(jnp.concatenate([trans, source], axis=1))


def with_source(moved, source):
    return jnp.concatenate([moved[:HEAD_DIM], moved[HEAD_DIM:] + source], axis=0)


def joined(first, later):
    moved = product(split(later), split(first[:HEAD_DIM]))
    return with_source(moved, first[HEAD_DIM:])


def row_kernel(maps_ref, total_ref, some_ref):
    maps = [decoded_map(maps_ref, n) for n in range(ROWS)]
    pairs = [joined(maps[n], maps[n + 1]) for n in range(0, ROWS, 2)]
    fours = [joined(pairs[0], pairs[1]), joined(pairs[2], pairs[3])]
    total = joined(fours[0], fours[1])
    trans, lines = coded_trans(total[:HEAD_DIM])
    source, scale = coded(total[HEAD_DIM:])
    notes = notes_of(lines[0], scale, *lines[1:])
    for n in range(ROWS):
        total_ref[n, :HEAD_DIM, :] = trans
        total_ref[n, HEAD_DIM:PACKET, :] = source
        total_ref[n, PACKET:, :] = notes
    some_ref[0] = pairs[1]
    some_ref[1] = pairs[3]
    some_ref[2] = fours[1]


def suffix_kernel(maps_ref, some_ref, suffix_ref):
    pair_second, pair_last, four_last = some_ref[0], some_ref[1], some_ref[2]
    suffix_ref[6] = decoded_map(maps_ref, 7)
    suffix_ref[5] = pair_last
    suffix_ref[4] = joined(decoded_map(maps_ref, 5), pair_last)
    suffix_ref[3] = four_last
    suffix_ref[2] = joined(decoded_map(maps_ref, 3), four_last)
    from_second = joined(pair_second, four_last)
    suffix_ref[1] = from_second
    suffix_ref[0] = joined(decoded_map(maps_ref, 1), from_second)


def state_kernel(place_ref, totals_ref, suffix_ref, states_ref):
    place = place_ref[0]
    row = lax.broadcasted_iota(jnp.int32, (PACKET, HEAD_DIM), 0)
    col = lax.broadcasted_iota(jnp.int32, (PACKET, HEAD_DIM), 1)
    identity = jnp.where(row == col, 1.0, 0.0)
    maps = [jnp.where(n > place, decoded_map(totals_ref, n), identity) for n in range(ROWS)]
    pairs = [joined(maps[n], maps[n + 1]) for n in (2, 4, 6)]
    front = joined(maps[1], pairs[0])
    back = joined(pairs[1], pairs[2])
    state = product(split(back[HEAD_DIM:]), split(front[:HEAD_DIM])) + front[HEAD_DIM:]
    states = [state]
    state = split(state)
    for n in reversed(range(ROWS - 1)):
        moved = product(state, split(suffix_ref[n, :HEAD_DIM, :]))
        states.append(moved + suffix_ref[n, HEAD_DIM:, :])
    for n, part in enumerate(reversed(states)):
        carrier, scale = coded(part)
        states_ref[n, :HALF, :] = carrier
        states_ref[n, HALF:, :] = notes_of(scale)


def result_kernel(gain_ref, own_ref, state_ref, out_ref):
    def against(left, right):
        return lax.dot_general(
            left, right, (((1,), (1,)), ((), ())), preferred_element_type=F32
        )

    for h in range(gain_ref.shape[0]):
        parts = [
            decoded(state_ref[n, :HALF, :], state_ref[n, HALF:, :].astype(F32)[0:1])
            for n in (2 * h, 2 * h + 1)
        ]
        high, low = split(jnp.concatenate(parts, axis=0))
        moved = against(gain_ref[h], jnp.concatenate([high, high], axis=1))
        moved = moved + against(gain_ref[h, :, :HEAD_DIM], low)
        out_ref[:, h * HEAD_DIM : (h + 1) * HEAD_DIM] = (own_ref[h] + moved).astype(BF16)


def params():
    return pltpu.CompilerParams(vmem_limit_bytes=40 * 1024 * 1024)


def in_vmem(shape, dtype=F32):
    return pl.BlockSpec(memory_space=pltpu.VMEM), jax.ShapeDtypeStruct(shape, dtype)


def in_hbm(shape, dtype=F32):
    return pl.BlockSpec(memory_space=pl.ANY), pltpu.HBM(shape, dtype)


def whole(kernel, outs, *args, first=pltpu.VMEM, scratch=()):
    specs = [pl.BlockSpec(memory_space=pltpu.VMEM)] * len(args)
    specs[0] = pl.BlockSpec(memory_space=first)
    return pl.pallas_call(
        kernel,
        in_specs=specs,
        out_specs=[spec for spec, _ in outs],
        out_shape=[shape for _, shape in outs],
        scratch_shapes=scratch,
        compiler_params=params(),
    )(*args)


def local(queries, keys, decay_log, write_rate, output_grad):
    heads, tokens = write_rate.shape
    devices = lax.axis_size("head")
    width = heads * HEAD_DIM
    part = devices // 2
    pieces = pl.pallas_call(
        pieces_kernel,
        grid=(2,),
        in_specs=[pl.BlockSpec((tokens // devices, part * width), lambda s: (0, s))],
        out_specs=pl.BlockSpec((part, tokens // devices, width), lambda s: (s, 0, 0)),
        out_shape=pltpu.HBM((devices, tokens // devices, width), BF16),
        compiler_params=params(),
    )(pltpu.with_memory_space_constraint(output_grad, pltpu.HBM))
    gathered = lax.all_to_all(pieces, "head", 0, 0, tiled=True).reshape(tokens, width)
    rates = write_rate.reshape(heads, 1, tokens)

    def blocks(count, *dims):
        return pl.BlockSpec((count,) + dims, lambda s: (s,) + (0,) * len(dims))

    def lanes(count):
        return pl.BlockSpec((tokens, count * HEAD_DIM), lambda s: (0, s))

    def by_heads(kernel, count, args, in_specs, outs):
        return pl.pallas_call(
            kernel,
            grid=(heads // count,),
            in_specs=in_specs,
            out_specs=[spec for spec, _ in outs],
            out_shape=[shape for _, shape in outs],
            compiler_params=params(),
        )(*args)

    def out(count, *dims, dtype=F32):
        return blocks(count, *dims), jax.ShapeDtypeStruct((heads,) + dims, dtype)

    tall_shape = (heads, tokens, HEAD_DIM)
    trans, lift, carry, reply, steps, sources = whole(
        maps_kernel,
        [in_vmem((heads, HEAD_DIM, HEAD_DIM)), in_vmem((heads, HEAD_DIM, tokens))]
        + [in_hbm(tall_shape)] * 4,
        queries,
        keys,
        decay_log,
        rates,
        scratch=[pltpu.VMEM(tall_shape, F32)] * 4 + [pltpu.SemaphoreType.DMA((4,))],
    )
    full, half = (ROWS, PACKET + NOTES, HEAD_DIM), (ROWS, HALF + NOTES, HEAD_DIM)
    (packet,) = whole(packet_kernel, [in_vmem(full, BF16)], trans, lift, gathered)
    maps = lax.all_to_all(packet, "y", 0, 0, tiled=True)
    tall = blocks(1, tokens, HEAD_DIM)
    gain, own = by_heads(
        answer_kernel,
        1,
        tuple(
            pltpu.with_memory_space_constraint(late, pltpu.HBM)
            for late in (carry, reply, steps, sources)
        )
        + (rates, gathered),
        [tall, tall, tall, tall, blocks(1, 1, tokens), lanes(1)],
        [out(1, tokens, 2 * HEAD_DIM, dtype=BF16), out(1, tokens, HEAD_DIM)],
    )
    total, some = whole(row_kernel, [in_vmem(full, BF16), in_vmem((3, PACKET, HEAD_DIM))], maps)
    totals = lax.all_to_all(total, "z", 0, 0, tiled=True)
    (suffix,) = whole(suffix_kernel, [in_vmem((ROWS - 1, PACKET, HEAD_DIM))], maps, some)
    totals, gain, own = lax.optimization_barrier((totals, gain, own))
    place = lax.axis_index("z").astype(jnp.int32).reshape(1)
    (states,) = whole(state_kernel, [in_vmem(half, BF16)], place, totals, suffix, first=pltpu.SMEM)
    states = lax.all_to_all(states, "y", 0, 0, tiled=True)
    (result,) = whole(result_kernel, [in_vmem((tokens, width), BF16)], gain, own, states)
    return result


def solution(mesh):
    seq, head = mesh.devices.shape
    grid = Mesh(mesh.devices.reshape(seq // ROWS, ROWS, head), ("z", "y", "head"))
    tokens = ("z", "y")
    return jax.shard_map(
        local,
        mesh=grid,
        in_specs=(
            P(tokens, "head"),
            P(tokens, "head"),
            P(tokens, "head"),
            P("head", tokens),
            P(("z", "y", "head"), None),
        ),
        out_specs=P(tokens, "head"),
        check_vma=False,
    )
```

```python
import jax
import jax.numpy as jnp
from jax import lax
from jax.experimental import pallas as pl
from jax.experimental.pallas import tpu as pltpu
from jax.sharding import Mesh, PartitionSpec as P

HEAD_DIM = 128
CHUNK = 128
HALF = 64
ROWS = 8
PACKET = HEAD_DIM + HALF
NOTES = 16
LEVELS = 31990.0
LOG_2 = 0.6931471805599453

epsilon = 1e-06
F32 = jnp.float32
BF16 = jnp.bfloat16


def split(values):
    high = values.astype(BF16)
    return high, (values - high.astype(F32)).astype(BF16)


def dot(left, right):
    return lax.dot_general(left, right, (((1,), (0,)), ((), ())), preferred_element_type=F32)


def product(left, right):
    left_high, left_low = left
    right_high, right_low = right
    both = jnp.concatenate([left_high, left_low], axis=1)
    width = right_high.shape[1]
    if width > HEAD_DIM:
        stacked = jnp.concatenate([right_high, right_high], axis=0)
        return dot(both, stacked) + dot(left_high, right_low)
    upper = jnp.concatenate([right_high, right_low], axis=1)
    lower = jnp.concatenate([right_high, jnp.zeros_like(right_low)], axis=1)
    parts = dot(both, jnp.concatenate([upper, lower], axis=0))
    return parts[:, :width] + parts[:, width:]


def exact_right(left, right):
    left_high, left_low = left
    both = jnp.concatenate([left_high, left_low], axis=1)
    return dot(both, jnp.concatenate([right, right], axis=0))


def indices(size):
    shape = (size, size)
    return lax.broadcasted_iota(jnp.int32, shape, 0), lax.broadcasted_iota(jnp.int32, shape, 1)


def unit_upper_inverses(strict_parts, row, col):
    size = row.shape[0]

    def above(parts, step):
        keep = (row // (2 * step) == col // (2 * step)) & (row // step < col // step)
        return [jnp.where(keep, part, 0.0) for part in parts]

    eye = jnp.where(row == col, 1.0, 0.0)
    inverses = [eye - part for part in above(strict_parts, 1)]
    step = 2
    while step < size:
        blocks = [split(part) for part in above(strict_parts, step)]
        pairs = [split(inverse) for inverse in inverses]
        if step < 8:
            left = [product(pair, block) for pair, block in zip(pairs, blocks)]
            left = [product(split(part), pair) for part, pair in zip(left, pairs)]
            inverses = [inverse - part for inverse, part in zip(inverses, left)]
        else:
            starts = range(0, size, 2 * step)
            upper = [
                split(jnp.concatenate([inverse[s : s + step] for s in starts], axis=0))
                for inverse in inverses
            ]
            left = [product(pair, block) for pair, block in zip(upper, blocks)]
            left = [product(split(part), pair) for part, pair in zip(left, pairs)]
            merged = []
            for inverse, part in zip(inverses, left):
                pieces = []
                for place, s in enumerate(starts):
                    pieces.append(
                        inverse[s : s + step] - part[place * step : (place + 1) * step]
                    )
                    pieces.append(inverse[s + step : s + 2 * step])
                merged.append(jnp.concatenate(pieces, axis=0))
            inverses = merged
        step = step * 2
    return inverses


def as_column(line, row, col):
    return jnp.sum(jnp.where(row == col, line, 0.0), axis=1, keepdims=True)


def maps_kernel(
    queries_ref, keys_ref, decay_ref, rate_ref,
    trans_ref, lift_ref, carry_out, reply_out, step_out, source_out,
    carry_ref, reply_ref, step_ref, source_ref, sems,
):
    row, col = indices(CHUNK)
    count = queries_ref.shape[0] // CHUNK
    heads = queries_ref.shape[1] // HEAD_DIM
    places = [
        (h, slice(n * CHUNK, (n + 1) * CHUNK), slice(h * HEAD_DIM, (h + 1) * HEAD_DIM))
        for h in range(heads)
        for n in range(count)
    ]
    lower = jnp.where(row >= col, 1.0, 0.0).astype(BF16)
    lower_twice = jnp.concatenate([lower, lower], axis=1)

    sums = []
    for _, chunk, lanes in places:
        decay = decay_ref[chunk, lanes]
        high, rest = split(decay)
        rest_value = decay - high.astype(F32) - rest.astype(F32)
        sums.append(
            dot(lower_twice, jnp.concatenate([high, rest], axis=0))
            + dot(lower, rest_value.astype(BF16))
        )
    ends = [jnp.exp(total[CHUNK - 1 :, :]) for total in sums]
    behind, ahead, carry = [], [], []
    for n, (h, chunk, lanes) in enumerate(places):
        keys = keys_ref[chunk, lanes].astype(F32)
        queries = queries_ref[chunk, lanes].astype(F32)
        keys_scale = lax.rsqrt(jnp.sum(keys * keys, axis=1, keepdims=True) + epsilon)
        queries_scale = lax.rsqrt(jnp.sum(queries * queries, axis=1, keepdims=True) + epsilon)
        rate = as_column(rate_ref[h, :, chunk], row, col)
        grown = jnp.exp(-sums[n])
        shrunk = jnp.exp(sums[n])
        keys = keys * keys_scale
        keys_behind = keys * grown
        behind.append(split(keys_behind))
        carry.append(keys_behind * ends[n])
        stacked = jnp.concatenate([keys * (shrunk * rate), queries * (shrunk * queries_scale)], axis=0)
        ahead.append(stacked.T)
    ahead_pairs = [split(part) for part in ahead]
    scores = [product(left, right) for left, right in zip(behind, ahead_pairs)]
    strict = [jnp.where(col > row, part[:, :CHUNK], 0.0) for part in scores]
    inverses = unit_upper_inverses(strict, row, col)
    solved = []
    for n in range(len(places)):
        queries_side = jnp.where(col >= row, scores[n][:, CHUNK:], 0.0)
        right = split(jnp.concatenate([queries_side, carry[n]], axis=1))
        solved.append(product(split(inverses[n]), right))
        h, chunk, _ = places[n]
        reply_ref[h, chunk, :] = solved[n][:, :CHUNK]
        carry_ref[h, chunk, :] = solved[n][:, CHUNK:]
    copies = [
        pltpu.make_async_copy(kept, late, sems.at[n])
        for n, (kept, late) in enumerate(
            [(carry_ref, carry_out), (reply_ref, reply_out),
             (step_ref, step_out), (source_ref, source_out)]
        )
    ]
    for copy in copies[:2]:
        copy.start()
    source, trans = [], []
    for n, (h, chunk, _) in enumerate(places):
        high, low = ahead_pairs[n]
        taken = product((high[:, :CHUNK], low[:, :CHUNK]), split(solved[n]))
        source.append(ahead[n][:, CHUNK:] - taken[:, :HEAD_DIM])
        trans.append(jnp.where(row == col, ends[n], 0.0) - taken[:, HEAD_DIM:])
        source_ref[h, chunk, :] = source[n]
        step_ref[h, chunk, :] = trans[n]
    for copy in copies[2:]:
        copy.start()
    parts = [(trans[n], [source[n]]) for n in range(len(places))]
    while len(parts) > heads:
        merged = []
        for n in range(0, len(parts), 2):
            first, later = parts[n], parts[n + 1]
            right = jnp.concatenate([later[0]] + later[1], axis=1)
            moved = product(split(first[0]), split(right))
            pieces = [moved[:, s : s + CHUNK] for s in range(HEAD_DIM, moved.shape[1], CHUNK)]
            merged.append((moved[:, :HEAD_DIM], first[1] + pieces))
        parts = merged
    for h, (turned, pieces) in enumerate(parts):
        trans_ref[h] = turned.T
        for n, part in enumerate(pieces):
            lift_ref[h, :, n * CHUNK : (n + 1) * CHUNK] = part
    for copy in copies:
        copy.wait()


def power_of_two(exponent):
    return jnp.exp(exponent * LOG_2)


def coded(values):
    scale = jnp.max(jnp.abs(values), axis=0, keepdims=True) * 1.01
    scale = jnp.maximum(scale.astype(BF16).astype(F32), 1e-30)
    steps = jnp.floor(jnp.abs(values) * (LEVELS / scale) + 0.5)
    exponent = jnp.floor(steps * (1.0 / 128.0))
    fraction = steps - exponent * 128.0
    carrier = (1.0 + fraction * (1.0 / 128.0)) * power_of_two(exponent - 125.0)
    return jnp.where(values < 0.0, -carrier, carrier).astype(BF16), scale


def decoded(carrier, scale):
    carrier = carrier.astype(F32)
    size = jnp.abs(carrier)
    exponent = jnp.floor(jnp.log(size * (1.0 + 1.0 / 512.0)) * (1.0 / LOG_2))
    fraction = jnp.floor((size * power_of_two(-exponent) - 1.0) * 128.0 + 0.5)
    steps = (exponent + 125.0) * 128.0 + fraction
    return jnp.where(carrier < 0.0, -steps, steps) * (scale * (1.0 / LEVELS))


def notes_of(*lines):
    pad = jnp.zeros((NOTES - len(lines), HEAD_DIM), F32)
    return jnp.concatenate(list(lines) + [pad], axis=0).astype(BF16)


def coded_trans(trans):
    row, col = indices(HEAD_DIM)
    diagonal = jnp.sum(jnp.where(row == col, trans, 0.0), axis=0, keepdims=True)
    carrier, scale = coded(jnp.where(row == col, 0.0, trans))
    high, middle = split(diagonal)
    high, middle = high.astype(F32), middle.astype(F32)
    return carrier, (scale, high, middle, diagonal - high - middle)


def decoded_map(ref, place):
    row, col = indices(HEAD_DIM)
    notes = ref[place, PACKET:, :].astype(F32)
    diagonal = notes[2:3] + notes[3:4] + notes[4:5]
    trans = decoded(ref[place, :HEAD_DIM, :], notes[0:1])
    source = decoded(ref[place, HEAD_DIM:PACKET, :], notes[1:2])
    return jnp.concatenate([jnp.where(row == col, diagonal, trans), source], axis=0)


def pieces_kernel(grads_ref, pieces_ref, sems):
    count, _, width = pieces_ref.shape
    copies = [
        pltpu.make_async_copy(
            grads_ref.at[:, n * width : (n + 1) * width], pieces_ref.at[n], sems.at[n]
        )
        for n in range(count)
    ]
    for copy in copies:
        copy.start()
    for copy in copies:
        copy.wait()


def packet_kernel(trans_ref, lift_ref, grads_ref, packet_ref):
    for h in range(trans_ref.shape[0]):
        grads = grads_ref[:, h * HEAD_DIM : (h + 1) * HEAD_DIM]
        source = exact_right(split(lift_ref[h]), grads).T
        trans, lines = coded_trans(trans_ref[h])
        for place in range(2):
            half, scale = coded(source[place * HALF : (place + 1) * HALF])
            packet_ref[2 * h + place, :HEAD_DIM, :] = trans
            packet_ref[2 * h + place, HEAD_DIM:PACKET, :] = half
            packet_ref[2 * h + place, PACKET:, :] = notes_of(lines[0], scale, *lines[1:])


def answer_kernel(
    carry_ref, reply_ref, step_ref, source_ref, rate_ref, grads_ref, gain_ref, own_ref
):
    row, col = indices(CHUNK)
    count = carry_ref.shape[1] // CHUNK
    chunks = [slice(n * CHUNK, (n + 1) * CHUNK) for n in range(count)]
    local = []
    for chunk in chunks:
        left = jnp.concatenate([reply_ref[0, chunk, :], source_ref[0, chunk, :]], axis=0)
        local.append(exact_right(split(left), grads_ref[chunk, :]))
    behind = None
    for n in reversed(range(count)):
        chunk = chunks[n]
        rate = as_column(rate_ref[0, :, chunk], row, col)
        own = local[n][:CHUNK]
        gain = carry_ref[0, chunk, :]
        if behind is not None:
            moved = product(split(gain), behind)
            gain = moved[:, :HEAD_DIM]
            own = own + moved[:, HEAD_DIM:]
        high, low = split(gain * rate)
        gain_ref[0, chunk, :HEAD_DIM] = high
        gain_ref[0, chunk, HEAD_DIM:] = low
        own_ref[0, chunk, :] = own * rate
        if n:
            trans = step_ref[0, chunk, :]
            source = local[n][CHUNK:]
            if behind is not None:
                moved = product(split(trans), behind)
                trans = moved[:, :HEAD_DIM]
                source = source + moved[:, HEAD_DIM:]
            behind = split(jnp.concatenate([trans, source], axis=1))


def with_source(moved, source):
    return jnp.concatenate([moved[:HEAD_DIM], moved[HEAD_DIM:] + source], axis=0)


def joined(first, later):
    moved = product(split(later), split(first[:HEAD_DIM]))
    return with_source(moved, first[HEAD_DIM:])


def row_kernel(maps_ref, total_ref, some_ref):
    maps = [decoded_map(maps_ref, n) for n in range(ROWS)]
    pairs = [joined(maps[n], maps[n + 1]) for n in range(0, ROWS, 2)]
    fours = [joined(pairs[0], pairs[1]), joined(pairs[2], pairs[3])]
    total = joined(fours[0], fours[1])
    trans, lines = coded_trans(total[:HEAD_DIM])
    source, scale = coded(total[HEAD_DIM:])
    notes = notes_of(lines[0], scale, *lines[1:])
    for n in range(ROWS):
        total_ref[n, :HEAD_DIM, :] = trans
        total_ref[n, HEAD_DIM:PACKET, :] = source
        total_ref[n, PACKET:, :] = notes
    some_ref[0] = pairs[1]
    some_ref[1] = pairs[3]
    some_ref[2] = fours[1]


def suffix_kernel(maps_ref, some_ref, suffix_ref):
    pair_second, pair_last, four_last = some_ref[0], some_ref[1], some_ref[2]
    suffix_ref[6] = decoded_map(maps_ref, 7)
    suffix_ref[5] = pair_last
    suffix_ref[4] = joined(decoded_map(maps_ref, 5), pair_last)
    suffix_ref[3] = four_last
    suffix_ref[2] = joined(decoded_map(maps_ref, 3), four_last)
    from_second = joined(pair_second, four_last)
    suffix_ref[1] = from_second
    suffix_ref[0] = joined(decoded_map(maps_ref, 1), from_second)


def state_kernel(place_ref, totals_ref, suffix_ref, states_ref):
    place = place_ref[0]
    row = lax.broadcasted_iota(jnp.int32, (PACKET, HEAD_DIM), 0)
    col = lax.broadcasted_iota(jnp.int32, (PACKET, HEAD_DIM), 1)
    identity = jnp.where(row == col, 1.0, 0.0)
    maps = [jnp.where(n > place, decoded_map(totals_ref, n), identity) for n in range(ROWS)]
    pairs = [joined(maps[n], maps[n + 1]) for n in (2, 4, 6)]
    front = joined(maps[1], pairs[0])
    back = joined(pairs[1], pairs[2])
    state = product(split(back[HEAD_DIM:]), split(front[:HEAD_DIM])) + front[HEAD_DIM:]
    states = [state]
    state = split(state)
    for n in reversed(range(ROWS - 1)):
        moved = product(state, split(suffix_ref[n, :HEAD_DIM, :]))
        states.append(moved + suffix_ref[n, HEAD_DIM:, :])
    for n, part in enumerate(reversed(states)):
        carrier, scale = coded(part)
        states_ref[n, :HALF, :] = carrier
        states_ref[n, HALF:, :] = notes_of(scale)


def result_kernel(gain_ref, own_ref, state_ref, out_ref):
    def against(left, right):
        return lax.dot_general(
            left, right, (((1,), (1,)), ((), ())), preferred_element_type=F32
        )

    for h in range(gain_ref.shape[0]):
        parts = [
            decoded(state_ref[n, :HALF, :], state_ref[n, HALF:, :].astype(F32)[0:1])
            for n in (2 * h, 2 * h + 1)
        ]
        high, low = split(jnp.concatenate(parts, axis=0))
        upper = jnp.concatenate([high, high], axis=1)
        lower = jnp.concatenate([low, jnp.zeros_like(low)], axis=1)
        moved = against(gain_ref[h], jnp.concatenate([upper, lower], axis=0))
        moved = moved[:, :HEAD_DIM] + moved[:, HEAD_DIM:]
        out_ref[:, h * HEAD_DIM : (h + 1) * HEAD_DIM] = (own_ref[h] + moved).astype(BF16)


def params():
    return pltpu.CompilerParams(vmem_limit_bytes=40 * 1024 * 1024)


def in_vmem(shape, dtype=F32):
    return pl.BlockSpec(memory_space=pltpu.VMEM), jax.ShapeDtypeStruct(shape, dtype)


def in_hbm(shape, dtype=F32):
    return pl.BlockSpec(memory_space=pl.ANY), pltpu.HBM(shape, dtype)


def whole(kernel, outs, *args, first=pltpu.VMEM, scratch=()):
    specs = [pl.BlockSpec(memory_space=pltpu.VMEM)] * len(args)
    specs[0] = pl.BlockSpec(memory_space=first)
    return pl.pallas_call(
        kernel,
        in_specs=specs,
        out_specs=[spec for spec, _ in outs],
        out_shape=[shape for _, shape in outs],
        scratch_shapes=scratch,
        compiler_params=params(),
    )(*args)


def local(queries, keys, decay_log, write_rate, output_grad):
    heads, tokens = write_rate.shape
    devices = lax.axis_size("head")
    width = heads * HEAD_DIM
    (pieces,) = whole(
        pieces_kernel,
        [in_vmem((devices, tokens // devices, width), BF16)],
        pltpu.with_memory_space_constraint(output_grad, pltpu.HBM),
        first=pltpu.HBM,
        scratch=[pltpu.SemaphoreType.DMA((devices,))],
    )
    gathered = lax.all_to_all(pieces, "head", 0, 0, tiled=True).reshape(tokens, width)
    rates = write_rate.reshape(heads, 1, tokens)

    def blocks(count, *dims):
        return pl.BlockSpec((count,) + dims, lambda s: (s,) + (0,) * len(dims))

    def lanes(count):
        return pl.BlockSpec((tokens, count * HEAD_DIM), lambda s: (0, s))

    def by_heads(kernel, count, args, in_specs, outs):
        return pl.pallas_call(
            kernel,
            grid=(heads // count,),
            in_specs=in_specs,
            out_specs=[spec for spec, _ in outs],
            out_shape=[shape for _, shape in outs],
            compiler_params=params(),
        )(*args)

    def out(count, *dims, dtype=F32):
        return blocks(count, *dims), jax.ShapeDtypeStruct((heads,) + dims, dtype)

    tall_shape = (heads, tokens, HEAD_DIM)
    trans, lift, carry, reply, steps, sources = whole(
        maps_kernel,
        [in_vmem((heads, HEAD_DIM, HEAD_DIM)), in_vmem((heads, HEAD_DIM, tokens))]
        + [in_hbm(tall_shape)] * 4,
        queries,
        keys,
        decay_log,
        rates,
        scratch=[pltpu.VMEM(tall_shape, F32)] * 4 + [pltpu.SemaphoreType.DMA((4,))],
    )
    full, half = (ROWS, PACKET + NOTES, HEAD_DIM), (ROWS, HALF + NOTES, HEAD_DIM)
    (packet,) = whole(packet_kernel, [in_vmem(full, BF16)], trans, lift, gathered)
    maps = lax.all_to_all(packet, "y", 0, 0, tiled=True)
    tall = blocks(1, tokens, HEAD_DIM)
    gain, own = by_heads(
        answer_kernel,
        1,
        tuple(
            pltpu.with_memory_space_constraint(late, pltpu.HBM)
            for late in (carry, reply, steps, sources)
        )
        + (rates, gathered),
        [tall, tall, tall, tall, blocks(1, 1, tokens), lanes(1)],
        [out(1, tokens, 2 * HEAD_DIM, dtype=BF16), out(1, tokens, HEAD_DIM)],
    )
    total, some = whole(row_kernel, [in_vmem(full, BF16), in_vmem((3, PACKET, HEAD_DIM))], maps)
    totals = lax.all_to_all(total, "z", 0, 0, tiled=True)
    (suffix,) = whole(suffix_kernel, [in_vmem((ROWS - 1, PACKET, HEAD_DIM))], maps, some)
    totals, gain, own = lax.optimization_barrier((totals, gain, own))
    place = lax.axis_index("z").astype(jnp.int32).reshape(1)
    (states,) = whole(state_kernel, [in_vmem(half, BF16)], place, totals, suffix, first=pltpu.SMEM)
    states = lax.all_to_all(states, "y", 0, 0, tiled=True)
    (result,) = whole(result_kernel, [in_vmem((tokens, width), BF16)], gain, own, states)
    return result


def solution(mesh):
    seq, head = mesh.devices.shape
    grid = Mesh(mesh.devices.reshape(seq // ROWS, ROWS, head), ("z", "y", "head"))
    tokens = ("z", "y")
    return jax.shard_map(
        local,
        mesh=grid,
        in_specs=(
            P(tokens, "head"),
            P(tokens, "head"),
            P(tokens, "head"),
            P("head", tokens),
            P(("z", "y", "head"), None),
        ),
        out_specs=P(tokens, "head"),
        check_vma=False,
    )
```

```python
import jax
import jax.numpy as jnp
from jax import lax
from jax.experimental import pallas as pl
from jax.experimental.pallas import tpu as pltpu
from jax.sharding import Mesh, PartitionSpec as P

HEAD_DIM = 128
CHUNK = 128
HALF = 64
ROWS = 8
PACKET = HEAD_DIM + HALF
NOTES = 16
LEVELS = 31990.0
LOG_2 = 0.6931471805599453

epsilon = 1e-06
F32 = jnp.float32
BF16 = jnp.bfloat16


def split(values):
    high = values.astype(BF16)
    return high, (values - high.astype(F32)).astype(BF16)


def dot(left, right):
    return lax.dot_general(left, right, (((1,), (0,)), ((), ())), preferred_element_type=F32)


def product(left, right):
    left_high, left_low = left
    right_high, right_low = right
    both = jnp.concatenate([left_high, left_low], axis=1)
    width = right_high.shape[1]
    if width > HEAD_DIM:
        stacked = jnp.concatenate([right_high, right_high], axis=0)
        return dot(both, stacked) + dot(left_high, right_low)
    upper = jnp.concatenate([right_high, right_low], axis=1)
    lower = jnp.concatenate([right_high, jnp.zeros_like(right_low)], axis=1)
    parts = dot(both, jnp.concatenate([upper, lower], axis=0))
    return parts[:, :width] + parts[:, width:]


def exact_right(left, right):
    left_high, left_low = left
    both = jnp.concatenate([left_high, left_low], axis=1)
    return dot(both, jnp.concatenate([right, right], axis=0))


def indices(size):
    shape = (size, size)
    return lax.broadcasted_iota(jnp.int32, shape, 0), lax.broadcasted_iota(jnp.int32, shape, 1)


def unit_upper_inverses(strict_parts, row, col):
    size = row.shape[0]

    def above(parts, step):
        keep = (row // (2 * step) == col // (2 * step)) & (row // step < col // step)
        return [jnp.where(keep, part, 0.0) for part in parts]

    eye = jnp.where(row == col, 1.0, 0.0)
    inverses = [eye - part for part in above(strict_parts, 1)]
    step = 2
    while step < size:
        blocks = [split(part) for part in above(strict_parts, step)]
        pairs = [split(inverse) for inverse in inverses]
        if step < 8:
            left = [product(pair, block) for pair, block in zip(pairs, blocks)]
            left = [product(split(part), pair) for part, pair in zip(left, pairs)]
            inverses = [inverse - part for inverse, part in zip(inverses, left)]
        else:
            starts = range(0, size, 2 * step)
            upper = [
                split(jnp.concatenate([inverse[s : s + step] for s in starts], axis=0))
                for inverse in inverses
            ]
            left = [product(pair, block) for pair, block in zip(upper, blocks)]
            left = [product(split(part), pair) for part, pair in zip(left, pairs)]
            merged = []
            for inverse, part in zip(inverses, left):
                pieces = []
                for place, s in enumerate(starts):
                    pieces.append(
                        inverse[s : s + step] - part[place * step : (place + 1) * step]
                    )
                    pieces.append(inverse[s + step : s + 2 * step])
                merged.append(jnp.concatenate(pieces, axis=0))
            inverses = merged
        step = step * 2
    return inverses


def as_column(line, row, col):
    return jnp.sum(jnp.where(row == col, line, 0.0), axis=1, keepdims=True)


def maps_kernel(
    queries_ref, keys_ref, decay_ref, rate_ref,
    trans_ref, lines_ref, lift_ref, carry_out, reply_out, step_out, source_out,
    carry_ref, reply_ref, step_ref, source_ref, sems,
):
    row, col = indices(CHUNK)
    count = queries_ref.shape[0] // CHUNK
    heads = queries_ref.shape[1] // HEAD_DIM
    places = [
        (h, slice(n * CHUNK, (n + 1) * CHUNK), slice(h * HEAD_DIM, (h + 1) * HEAD_DIM))
        for h in range(heads)
        for n in range(count)
    ]
    lower = jnp.where(row >= col, 1.0, 0.0).astype(BF16)
    lower_twice = jnp.concatenate([lower, lower], axis=1)

    sums = []
    for _, chunk, lanes in places:
        decay = decay_ref[chunk, lanes]
        high, rest = split(decay)
        rest_value = decay - high.astype(F32) - rest.astype(F32)
        sums.append(
            dot(lower_twice, jnp.concatenate([high, rest], axis=0))
            + dot(lower, rest_value.astype(BF16))
        )
    ends = [jnp.exp(total[CHUNK - 1 :, :]) for total in sums]
    behind, ahead, carry = [], [], []
    for n, (h, chunk, lanes) in enumerate(places):
        keys = keys_ref[chunk, lanes].astype(F32)
        queries = queries_ref[chunk, lanes].astype(F32)
        keys_scale = lax.rsqrt(jnp.sum(keys * keys, axis=1, keepdims=True) + epsilon)
        queries_scale = lax.rsqrt(jnp.sum(queries * queries, axis=1, keepdims=True) + epsilon)
        rate = as_column(rate_ref[h, :, chunk], row, col)
        grown = jnp.exp(-sums[n])
        shrunk = jnp.exp(sums[n])
        keys = keys * keys_scale
        keys_behind = keys * grown
        behind.append(split(keys_behind))
        carry.append(keys_behind * ends[n])
        stacked = jnp.concatenate([keys * (shrunk * rate), queries * (shrunk * queries_scale)], axis=0)
        ahead.append(stacked.T)
    ahead_pairs = [split(part) for part in ahead]
    scores = [product(left, right) for left, right in zip(behind, ahead_pairs)]
    strict = [jnp.where(col > row, part[:, :CHUNK], 0.0) for part in scores]
    inverses = unit_upper_inverses(strict, row, col)
    solved = []
    for n in range(len(places)):
        queries_side = jnp.where(col >= row, scores[n][:, CHUNK:], 0.0)
        right = split(jnp.concatenate([queries_side, carry[n]], axis=1))
        solved.append(product(split(inverses[n]), right))
        h, chunk, _ = places[n]
        reply_ref[h, chunk, :] = solved[n][:, :CHUNK]
        carry_ref[h, chunk, :] = solved[n][:, CHUNK:]
    copies = [
        pltpu.make_async_copy(kept, late, sems.at[n])
        for n, (kept, late) in enumerate(
            [(carry_ref, carry_out), (reply_ref, reply_out),
             (step_ref, step_out), (source_ref, source_out)]
        )
    ]
    for copy in copies[:2]:
        copy.start()
    source, trans = [], []
    for n, (h, chunk, _) in enumerate(places):
        high, low = ahead_pairs[n]
        taken = product((high[:, :CHUNK], low[:, :CHUNK]), split(solved[n]))
        source.append(ahead[n][:, CHUNK:] - taken[:, :HEAD_DIM])
        trans.append(jnp.where(row == col, ends[n], 0.0) - taken[:, HEAD_DIM:])
        source_ref[h, chunk, :] = source[n]
        step_ref[h, chunk, :] = trans[n]
    for copy in copies[2:]:
        copy.start()
    parts = [(trans[n], [source[n]]) for n in range(len(places))]
    while len(parts) > heads:
        merged = []
        for n in range(0, len(parts), 2):
            first, later = parts[n], parts[n + 1]
            right = jnp.concatenate([later[0]] + later[1], axis=1)
            moved = product(split(first[0]), split(right))
            pieces = [moved[:, s : s + CHUNK] for s in range(HEAD_DIM, moved.shape[1], CHUNK)]
            merged.append((moved[:, :HEAD_DIM], first[1] + pieces))
        parts = merged
    for h, (turned, pieces) in enumerate(parts):
        trans_ref[h], lines = coded_trans(turned.T)
        lines_ref[h, : len(lines), :] = jnp.concatenate(lines, axis=0)
        width = len(pieces) * CHUNK
        for n, part in enumerate(pieces):
            high, low = split(part)
            lift_ref[h, :, n * CHUNK : (n + 1) * CHUNK] = high
            lift_ref[h, :, width + n * CHUNK : width + (n + 1) * CHUNK] = low
    for copy in copies:
        copy.wait()


def power_of_two(exponent):
    return jnp.exp(exponent * LOG_2)


def coded(values):
    scale = jnp.max(jnp.abs(values), axis=0, keepdims=True) * 1.01
    scale = jnp.maximum(scale.astype(BF16).astype(F32), 1e-30)
    steps = jnp.floor(jnp.abs(values) * (LEVELS / scale) + 0.5)
    exponent = jnp.floor(steps * (1.0 / 128.0))
    fraction = steps - exponent * 128.0
    carrier = (1.0 + fraction * (1.0 / 128.0)) * power_of_two(exponent - 125.0)
    return jnp.where(values < 0.0, -carrier, carrier).astype(BF16), scale


def decoded(carrier, scale):
    carrier = carrier.astype(F32)
    size = jnp.abs(carrier)
    exponent = jnp.floor(jnp.log(size * (1.0 + 1.0 / 512.0)) * (1.0 / LOG_2))
    fraction = jnp.floor((size * power_of_two(-exponent) - 1.0) * 128.0 + 0.5)
    steps = (exponent + 125.0) * 128.0 + fraction
    return jnp.where(carrier < 0.0, -steps, steps) * (scale * (1.0 / LEVELS))


def notes_of(*lines):
    pad = jnp.zeros((NOTES - len(lines), HEAD_DIM), F32)
    return jnp.concatenate(list(lines) + [pad], axis=0).astype(BF16)


def coded_trans(trans):
    row, col = indices(HEAD_DIM)
    diagonal = jnp.sum(jnp.where(row == col, trans, 0.0), axis=0, keepdims=True)
    carrier, scale = coded(jnp.where(row == col, 0.0, trans))
    high, middle = split(diagonal)
    high, middle = high.astype(F32), middle.astype(F32)
    return carrier, (scale, high, middle, diagonal - high - middle)


def decoded_map(ref, place):
    row, col = indices(HEAD_DIM)
    notes = ref[place, PACKET:, :].astype(F32)
    diagonal = notes[2:3] + notes[3:4] + notes[4:5]
    trans = decoded(ref[place, :HEAD_DIM, :], notes[0:1])
    source = decoded(ref[place, HEAD_DIM:PACKET, :], notes[1:2])
    return jnp.concatenate([jnp.where(row == col, diagonal, trans), source], axis=0)


def pieces_kernel(grads_ref, pieces_ref, sems):
    count, _, width = pieces_ref.shape
    copies = [
        pltpu.make_async_copy(
            grads_ref.at[:, n * width : (n + 1) * width], pieces_ref.at[n], sems.at[n]
        )
        for n in range(count)
    ]
    for copy in copies:
        copy.start()
    for copy in copies:
        copy.wait()


def packet_kernel(trans_ref, lines_ref, lift_ref, grads_ref, packet_ref):
    for h in range(trans_ref.shape[0]):
        grads = grads_ref[:, h * HEAD_DIM : (h + 1) * HEAD_DIM]
        source = dot(lift_ref[h], jnp.concatenate([grads, grads], axis=0)).T
        lines = [lines_ref[h, n : n + 1, :] for n in range(4)]
        for place in range(2):
            half, scale = coded(source[place * HALF : (place + 1) * HALF])
            packet_ref[2 * h + place, :HEAD_DIM, :] = trans_ref[h]
            packet_ref[2 * h + place, HEAD_DIM:PACKET, :] = half
            packet_ref[2 * h + place, PACKET:, :] = notes_of(lines[0], scale, *lines[1:])


def answer_kernel(
    carry_ref, reply_ref, step_ref, source_ref, rate_ref, grads_ref, gain_ref, own_ref
):
    row, col = indices(CHUNK)
    count = carry_ref.shape[1] // CHUNK
    chunks = [slice(n * CHUNK, (n + 1) * CHUNK) for n in range(count)]
    local = []
    for chunk in chunks:
        left = jnp.concatenate([reply_ref[0, chunk, :], source_ref[0, chunk, :]], axis=0)
        local.append(exact_right(split(left), grads_ref[chunk, :]))
    behind = None
    for n in reversed(range(count)):
        chunk = chunks[n]
        rate = as_column(rate_ref[0, :, chunk], row, col)
        own = local[n][:CHUNK]
        gain = carry_ref[0, chunk, :]
        if behind is not None:
            moved = product(split(gain), behind)
            gain = moved[:, :HEAD_DIM]
            own = own + moved[:, HEAD_DIM:]
        high, low = split(gain * rate)
        gain_ref[0, chunk, :HEAD_DIM] = high
        gain_ref[0, chunk, HEAD_DIM:] = low
        own_ref[0, chunk, :] = own * rate
        if n:
            trans = step_ref[0, chunk, :]
            source = local[n][CHUNK:]
            if behind is not None:
                moved = product(split(trans), behind)
                trans = moved[:, :HEAD_DIM]
                source = source + moved[:, HEAD_DIM:]
            behind = split(jnp.concatenate([trans, source], axis=1))


def with_source(moved, source):
    return jnp.concatenate([moved[:HEAD_DIM], moved[HEAD_DIM:] + source], axis=0)


def joined(first, later):
    moved = product(split(later), split(first[:HEAD_DIM]))
    return with_source(moved, first[HEAD_DIM:])


def row_kernel(maps_ref, total_ref, some_ref):
    maps = [decoded_map(maps_ref, n) for n in range(ROWS)]
    pairs = [joined(maps[n], maps[n + 1]) for n in range(0, ROWS, 2)]
    fours = [joined(pairs[0], pairs[1]), joined(pairs[2], pairs[3])]
    total = joined(fours[0], fours[1])
    trans, lines = coded_trans(total[:HEAD_DIM])
    source, scale = coded(total[HEAD_DIM:])
    notes = notes_of(lines[0], scale, *lines[1:])
    for n in range(ROWS):
        total_ref[n, :HEAD_DIM, :] = trans
        total_ref[n, HEAD_DIM:PACKET, :] = source
        total_ref[n, PACKET:, :] = notes
    some_ref[0] = pairs[1]
    some_ref[1] = pairs[3]
    some_ref[2] = fours[1]


def suffix_kernel(maps_ref, some_ref, trans_ref, source_ref):
    pair_second, pair_last, four_last = some_ref[0], some_ref[1], some_ref[2]
    from_second = joined(pair_second, four_last)
    suffixes = [
        joined(decoded_map(maps_ref, 1), from_second),
        from_second,
        joined(decoded_map(maps_ref, 3), four_last),
        four_last,
        joined(decoded_map(maps_ref, 5), pair_last),
        pair_last,
        decoded_map(maps_ref, 7),
    ]
    for n, part in enumerate(suffixes):
        trans_ref[n, :HEAD_DIM, :], trans_ref[n, HEAD_DIM:, :] = split(part[:HEAD_DIM])
        source_ref[n] = part[HEAD_DIM:]


def state_kernel(place_ref, totals_ref, trans_ref, source_ref, states_ref):
    place = place_ref[0]
    row = lax.broadcasted_iota(jnp.int32, (PACKET, HEAD_DIM), 0)
    col = lax.broadcasted_iota(jnp.int32, (PACKET, HEAD_DIM), 1)
    identity = jnp.where(row == col, 1.0, 0.0)
    maps = [jnp.where(n > place, decoded_map(totals_ref, n), identity) for n in range(ROWS)]
    pairs = [joined(maps[n], maps[n + 1]) for n in (2, 4, 6)]
    front = joined(maps[1], pairs[0])
    back = joined(pairs[1], pairs[2])
    state = product(split(back[HEAD_DIM:]), split(front[:HEAD_DIM])) + front[HEAD_DIM:]
    states = [state]
    state = split(state)
    for n in reversed(range(ROWS - 1)):
        moved = product(state, (trans_ref[n, :HEAD_DIM, :], trans_ref[n, HEAD_DIM:, :]))
        states.append(moved + source_ref[n])
    for n, part in enumerate(reversed(states)):
        carrier, scale = coded(part)
        states_ref[n, :HALF, :] = carrier
        states_ref[n, HALF:, :] = notes_of(scale)


def result_kernel(gain_ref, own_ref, state_ref, out_ref):
    def against(left, right):
        return lax.dot_general(
            left, right, (((1,), (1,)), ((), ())), preferred_element_type=F32
        )

    for h in range(gain_ref.shape[0]):
        parts = [
            decoded(state_ref[n, :HALF, :], state_ref[n, HALF:, :].astype(F32)[0:1])
            for n in (2 * h, 2 * h + 1)
        ]
        high, low = split(jnp.concatenate(parts, axis=0))
        upper = jnp.concatenate([high, high], axis=1)
        lower = jnp.concatenate([low, jnp.zeros_like(low)], axis=1)
        moved = against(gain_ref[h], jnp.concatenate([upper, lower], axis=0))
        moved = moved[:, :HEAD_DIM] + moved[:, HEAD_DIM:]
        out_ref[:, h * HEAD_DIM : (h + 1) * HEAD_DIM] = (own_ref[h] + moved).astype(BF16)


def params():
    return pltpu.CompilerParams(vmem_limit_bytes=40 * 1024 * 1024)


def in_vmem(shape, dtype=F32):
    return pl.BlockSpec(memory_space=pltpu.VMEM), jax.ShapeDtypeStruct(shape, dtype)


def in_hbm(shape, dtype=F32):
    return pl.BlockSpec(memory_space=pl.ANY), pltpu.HBM(shape, dtype)


def whole(kernel, outs, *args, first=pltpu.VMEM, scratch=()):
    specs = [pl.BlockSpec(memory_space=pltpu.VMEM)] * len(args)
    specs[0] = pl.BlockSpec(memory_space=first)
    return pl.pallas_call(
        kernel,
        in_specs=specs,
        out_specs=[spec for spec, _ in outs],
        out_shape=[shape for _, shape in outs],
        scratch_shapes=scratch,
        compiler_params=params(),
    )(*args)


def local(queries, keys, decay_log, write_rate, output_grad):
    heads, tokens = write_rate.shape
    devices = lax.axis_size("head")
    width = heads * HEAD_DIM
    (pieces,) = whole(
        pieces_kernel,
        [in_vmem((devices, tokens // devices, width), BF16)],
        pltpu.with_memory_space_constraint(output_grad, pltpu.HBM),
        first=pltpu.HBM,
        scratch=[pltpu.SemaphoreType.DMA((devices,))],
    )
    gathered = lax.all_to_all(pieces, "head", 0, 0, tiled=True).reshape(tokens, width)
    rates = write_rate.reshape(heads, 1, tokens)

    def blocks(count, *dims):
        return pl.BlockSpec((count,) + dims, lambda s: (s,) + (0,) * len(dims))

    def lanes(count):
        return pl.BlockSpec((tokens, count * HEAD_DIM), lambda s: (0, s))

    def by_heads(kernel, count, args, in_specs, outs):
        return pl.pallas_call(
            kernel,
            grid=(heads // count,),
            in_specs=in_specs,
            out_specs=[spec for spec, _ in outs],
            out_shape=[shape for _, shape in outs],
            compiler_params=params(),
        )(*args)

    def out(count, *dims, dtype=F32):
        return blocks(count, *dims), jax.ShapeDtypeStruct((heads,) + dims, dtype)

    tall_shape = (heads, tokens, HEAD_DIM)
    trans, lines, lift, carry, reply, steps, sources = whole(
        maps_kernel,
        [
            in_vmem((heads, HEAD_DIM, HEAD_DIM), BF16),
            in_vmem((heads, 8, HEAD_DIM)),
            in_vmem((heads, HEAD_DIM, 2 * tokens), BF16),
        ]
        + [in_hbm(tall_shape)] * 4,
        queries,
        keys,
        decay_log,
        rates,
        scratch=[pltpu.VMEM(tall_shape, F32)] * 4 + [pltpu.SemaphoreType.DMA((4,))],
    )
    full, half = (ROWS, PACKET + NOTES, HEAD_DIM), (ROWS, HALF + NOTES, HEAD_DIM)
    (packet,) = whole(packet_kernel, [in_vmem(full, BF16)], trans, lines, lift, gathered)
    maps = lax.all_to_all(packet, "y", 0, 0, tiled=True)
    tall = blocks(1, tokens, HEAD_DIM)
    gain, own = by_heads(
        answer_kernel,
        1,
        tuple(
            pltpu.with_memory_space_constraint(late, pltpu.HBM)
            for late in (carry, reply, steps, sources)
        )
        + (rates, gathered),
        [tall, tall, tall, tall, blocks(1, 1, tokens), lanes(1)],
        [out(1, tokens, 2 * HEAD_DIM, dtype=BF16), out(1, tokens, HEAD_DIM)],
    )
    total, some = whole(row_kernel, [in_vmem(full, BF16), in_vmem((3, PACKET, HEAD_DIM))], maps)
    totals = lax.all_to_all(total, "z", 0, 0, tiled=True)
    suffix = whole(
        suffix_kernel,
        [in_vmem((ROWS - 1, 2 * HEAD_DIM, HEAD_DIM), BF16), in_vmem((ROWS - 1, HALF, HEAD_DIM))],
        maps,
        some,
    )
    totals, gain, own = lax.optimization_barrier((totals, gain, own))
    place = lax.axis_index("z").astype(jnp.int32).reshape(1)
    (states,) = whole(state_kernel, [in_vmem(half, BF16)], place, totals, *suffix, first=pltpu.SMEM)
    states = lax.all_to_all(states, "y", 0, 0, tiled=True)
    (result,) = whole(result_kernel, [in_vmem((tokens, width), BF16)], gain, own, states)
    return result


def solution(mesh):
    seq, head = mesh.devices.shape
    grid = Mesh(mesh.devices.reshape(seq // ROWS, ROWS, head), ("z", "y", "head"))
    tokens = ("z", "y")
    return jax.shard_map(
        local,
        mesh=grid,
        in_specs=(
            P(tokens, "head"),
            P(tokens, "head"),
            P(tokens, "head"),
            P("head", tokens),
            P(("z", "y", "head"), None),
        ),
        out_specs=P(tokens, "head"),
        check_vma=False,
    )
```
